32 devices in a mesh: groups: 2 (over x), replica: 4 (over y, core), tensor: 4 (over z).
Axes of the slice: x: 2, y: 2, z: 4, core: 2. Of those that a mesh axis runs over, the one named last changes fastest.
Arguments:
- tokens: bfloat16 [128, 5120], P('groups', 'replica'), parts along dimension 0, may hold values from -6 to 6
- gate_matrix: bfloat16 [5120, 25600], P('replica', 'tensor'), may hold values from -0.078125 to 0.078125
- up_matrix: bfloat16 [5120, 25600], P('replica', 'tensor'), may hold values from -0.078125 to 0.078125
- down_weight: bfloat16 [25600, 5120], P('tensor', 'replica'), may hold values from -0.0390625 to 0.0390625
- adapter_down: bfloat16 [32, 2, 16, 5120], P('replica'), may hold values from -0.078125 to 0.078125
- adapter_up: bfloat16 [32, 2, 16, 25600], P('replica', None, None, 'tensor'), may hold values from -1.5 to 1.5
- adapter_ids: int32 [128], P('groups'), parts along dimension 0, may hold values from 0 to 31, as said below
- adapter_slot: int32 [64], P('groups'), parts along dimension 0, may hold values from 0 to 31, as said below
Outputs:
- layer_output: bfloat16 [128, 5120], P('groups', 'replica'), parts along dimension 0
The draws below stay inside these ranges and needn't reach their ends.
There are 2 independent parts, one for each index of `groups`. The reference program is written for one: setup_inputs(seed, part) draws one part's arguments, and reference() takes and returns one part's arrays. A program takes and returns all parts, laid end to end along the dimension named above; an argument that names none is the same for every part. Nothing has to cross between parts.
Inputs may be any that keep to these rules, and one draw needn't show every extreme that they name: `adapter_ids`: adapter a is stored in slot adapter_slot[a]; slots s * 8 to (s + 1) * 8 - 1 are those of index s of replica. In each aligned block of 16 rows, at most 8 rows use adapters stored on one index of replica, and in every block some index gets exactly 8. `adapter_slot`: A permutation of the adapters' slots.
All inputs are finite; a program needn't handle non-finite values.
Results may differ from the reference program's by a relative error of at most 0.0056.
Values may be sent and summed in bfloat16 or wider, within the bound.
No kernel may reach another device: no remote copies, remote signals or barrier semaphores. Data moves between devices by JAX's collectives and lax.ppermute only.
A program may use at most 128 MiB of HBM per device.

```python
import jax
import jax.numpy as jnp
from jax import lax

MODEL_WIDTH = 5120
HIDDEN_UNITS = 25600
RANK = 16
ALIGNED_ROWS = 16
ADP_REP = 8
BATCH_ROWS = 64
ADAPTERS = 32
CAP = 8
N_REPLICA = 4


def slot_table(key):
    return jax.random.permutation(jax.random.fold_in(key, 11), ADAPTERS).astype(jnp.int32)


def draw_adapter_slot(key, part):
    placed = slot_table(key)
    return placed


def block_owners(block_key, favored):
    key_list = jax.random.split(block_key, 4)
    slot_total = N_REPLICA * CAP
    noise = jax.random.randint(key_list[0], (slot_total,), 0, 4096)
    score = (noise + 4096 * favored) * slot_total + jnp.arange(slot_total, dtype=jnp.int32)
    ordering = jnp.argsort(-score, stable=True)
    owner_of_slot = jnp.arange(slot_total, dtype=jnp.int32) // CAP
    chosen = owner_of_slot[ordering[:ALIGNED_ROWS]]
    shuffled = chosen[jax.random.permutation(key_list[1], ALIGNED_ROWS)]
    first_pick = jax.random.randint(key_list[2], (ALIGNED_ROWS,), 0, ADP_REP)
    second_pick = jax.random.randint(key_list[3], (ALIGNED_ROWS,), 0, ADP_REP)
    return shuffled * ADP_REP + jnp.minimum(first_pick, second_pick)


def draw_adapter_ids(key, part):
    placed = slot_table(key)
    key = jax.random.fold_in(key, 5)
    hot_count = max(1, N_REPLICA // 4)
    owner_rank = jax.random.permutation(jax.random.fold_in(key, 1), N_REPLICA)
    favored = (owner_rank[jnp.arange(N_REPLICA * CAP) // CAP] < hot_count).astype(jnp.int32)
    block_keys = jax.random.split(jax.random.fold_in(key, 2), N_REPLICA)
    storage = jax.vmap(lambda block_key: block_owners(block_key, favored))(block_keys)
    holder = jnp.argsort(placed, stable=True).astype(jnp.int32)
    return holder[storage.reshape(BATCH_ROWS)].astype(jnp.int32)


def block_levels(key, shape, shards, low, high):
    def one(dim, blocks):
        draws = jax.random.uniform(jax.random.fold_in(jax.random.fold_in(key, 6), dim), (blocks,), jnp.float32, low / len(shards), high / len(shards))
        return jnp.repeat(jnp.exp(draws), shape[dim] // blocks).reshape((-1,) + (1,) * (len(shape) - dim - 1))

    loudness = one(*shards[0])
    for cut in shards[1:]:
        loudness = loudness * one(*cut)
    return loudness


def scatter_about(rng, shape, spread, reach, shards=(), kind=jnp.bfloat16):
    array = jax.random.normal(rng, shape, jnp.float32) * spread
    if len(shards) > 0:
        array = block_levels(rng, shape, shards, -0.22, 0.18) * array
    return jnp.clip(array, min=-reach, max=reach).astype(kind)


def setup_inputs(seed: int = 0, part: int = 0) -> dict:
    streams_of = jax.random.split(jax.random.key(seed), 9)
    part_keys = jax.random.split(jax.random.fold_in(streams_of[8], part), 9)
    return {
        "tokens": scatter_about(part_keys[0], (BATCH_ROWS, MODEL_WIDTH), 1.0, 6.0, ((1, 4),)),
        "gate_matrix": scatter_about(streams_of[1], (MODEL_WIDTH, HIDDEN_UNITS), MODEL_WIDTH ** -0.5, 0.078125, ((0, 4), (1, 4))),
        "up_matrix": scatter_about(streams_of[2], (MODEL_WIDTH, HIDDEN_UNITS), MODEL_WIDTH ** -0.5, 0.078125, ((0, 4), (1, 4))),
        "down_weight": scatter_about(streams_of[3], (HIDDEN_UNITS, MODEL_WIDTH), HIDDEN_UNITS ** -0.5, 0.0390625, ((0, 4), (1, 4))),
        "adapter_down": scatter_about(streams_of[4], (ADAPTERS, 2, RANK, MODEL_WIDTH), MODEL_WIDTH ** -0.5, 0.078125, ((0, 4),)),
        "adapter_up": scatter_about(streams_of[5], (ADAPTERS, 2, RANK, HIDDEN_UNITS), RANK ** -0.5, 1.5, ((0, 4), (3, 4))),
        "adapter_ids": draw_adapter_ids(jax.random.fold_in(jax.random.fold_in(streams_of[8], part), 71), part),
        "adapter_slot": draw_adapter_slot(jax.random.fold_in(jax.random.fold_in(streams_of[8], part), 71), part),
    }


low_rank_scale = 0.5


def reference(tokens, gate_matrix, up_matrix, down_weight, adapter_down, adapter_up, adapter_ids, adapter_slot):
    row_slot_lookup = jnp.take(adapter_slot, adapter_ids, axis=0).astype(jnp.int32)

    def delta_of_block(packed):
        row_block, slot_block = packed
        down_rows = jnp.take(adapter_down, slot_block, axis=0).astype(jnp.float32)
        shrink = jnp.einsum("bd,bprd->bpr", row_block.astype(jnp.float32), down_rows).astype(jnp.bfloat16)
        up_rows = jnp.take(adapter_up, slot_block, axis=0).astype(jnp.float32)
        dispersed = jnp.einsum("bpr,bprf->bpf", shrink.astype(jnp.float32), up_rows)
        return (low_rank_scale * dispersed).astype(jnp.bfloat16)

    low_rank_delta = lax.map(delta_of_block, (tokens.reshape(-1, ALIGNED_ROWS, MODEL_WIDTH), row_slot_lookup.reshape(-1, ALIGNED_ROWS)))
    low_rank_delta = low_rank_delta.reshape(BATCH_ROWS, 2, HIDDEN_UNITS).astype(jnp.float32)
    gate_totals = jnp.dot(tokens, gate_matrix, preferred_element_type=jnp.float32) + low_rank_delta[:, 0]
    up_totals = jnp.dot(tokens, up_matrix, preferred_element_type=jnp.float32) + low_rank_delta[:, 1]
    hidden = (jax.nn.silu(gate_totals) * up_totals).astype(jnp.bfloat16)
    return jnp.dot(hidden, down_weight, preferred_element_type=jnp.float32).astype(jnp.bfloat16)
```

```python
import jax
import jax.numpy as jnp
from jax import lax
from jax.experimental import pallas as pl
from jax.experimental.pallas import tpu as pltpu
from jax.sharding import PartitionSpec as P

low_rank_scale = 0.5
f32 = jnp.float32
bf16 = jnp.bfloat16
MIB = 1 << 20
CHUNKS = (1280, 1280, 1280, 1280, 1280)
GATHERED = False


def dot(a, b):
    return jnp.dot(a, b, preferred_element_type=f32)


def core_swap(value, replicas):
    return lax.ppermute(value, "replica", [(i, i ^ 1) for i in range(replicas)])


def from_chip(value, replicas, step, flip=0):
    pairs = [((i + 2 * step) % replicas ^ flip, i) for i in range(replicas)]
    return lax.ppermute(value, "replica", pairs)


def shrink_kernel(source_ref, ids_ref, slots_ref, order_ref, down_ref, *refs):
    pieces, spread_ref = refs[:-1], refs[-1]
    rows, width = pieces[0].shape
    stored, _, rank, full = down_ref.shape
    table = stored * 2 * rank
    total = jnp.zeros((rows, table), f32)
    for j, piece in enumerate(pieces):
        columns = pl.ds(pl.multiple_of(source_ref[j] * width, 128), width)
        part = down_ref[:, :, :, columns].reshape(table, width)
        total += lax.dot_general(piece[...], part, (((1,), (1,)), ((), ())), preferred_element_type=f32)
    shrink = total.astype(bf16).astype(f32)
    ids = ids_ref[...]
    known = lax.broadcasted_iota(jnp.int32, (rows, slots_ref.shape[1]), 1)
    slot = jnp.sum(jnp.where(ids == known, slots_ref[...], 0), axis=1, keepdims=True)
    local = slot - source_ref[len(pieces)] * stored
    column = lax.broadcasted_iota(jnp.int32, (rows, table), 1)
    for p in range(2):
        first = local * (2 * rank) + p * rank
        mine = jnp.logical_and(column >= first, column < first + rank)
        picked = jnp.where(mine, shrink, 0.0).astype(bf16)
        spread_ref[p] = dot(order_ref[...], picked).astype(bf16)


def shrink_rows(pieces, sources, ids, slots, order, adapter_down):
    rows = ids.shape[0]
    stored, _, rank, _ = adapter_down.shape
    vmem = pl.BlockSpec(memory_space=pltpu.VMEM)
    return pl.pallas_call(
        shrink_kernel,
        out_shape=jax.ShapeDtypeStruct((2, rows, stored * 2 * rank), bf16),
        in_specs=[pl.BlockSpec(memory_space=pltpu.SMEM)] + [vmem] * (4 + len(pieces)),
        out_specs=vmem,
        compiler_params=pltpu.CompilerParams(vmem_limit_bytes=24 * MIB),
        cost_estimate=pl.CostEstimate(
            flops=2 * adapter_down.size * rows, bytes_accessed=2 * adapter_down.size, transcendentals=0
        ),
        name="shrink",
    )(sources, ids.reshape(rows, 1), slots.reshape(1, -1), order, adapter_down, *pieces)


def shards(
    tokens, gate_matrix, up_matrix, down_weight, adapter_down, adapter_up, adapter_ids, adapter_slot
):
    replicas, depth = lax.axis_size("replica"), lax.axis_size("tensor")
    chips = replicas // 2
    me, layer = lax.axis_index("replica"), lax.axis_index("tensor")
    rows = tokens.shape[0]
    block = rows // replicas
    half = rows // 2
    units = gate_matrix.shape[1]
    place = jnp.arange(rows, dtype=jnp.int32)
    nth, within = place // block, place % block
    chip = (me // 2 + nth % chips) % chips
    natural = (chip * 2 + ((me % 2) ^ (nth // chips))) * block + within
    order = (natural[:, None] == place[None, :]).astype(bf16)

    pieces = [tokens, core_swap(tokens, replicas)]
    sources = [me, me ^ 1]
    for step in range(1, chips):
        for flip in range(2):
            pieces.append(from_chip(tokens, replicas, step, flip))
            sources.append((me + 2 * step) % replicas ^ flip)
    mixed = dot(order, tokens).astype(bf16)
    spread = shrink_rows(
        pieces, jnp.stack(sources + [me]).astype(jnp.int32), adapter_ids, adapter_slot, order, adapter_down
    )
    expand = adapter_up.reshape(-1, units)

    widths = CHUNKS if sum(CHUNKS) == units else (units,)
    total = None
    start = 0
    for width in widths:
        cut = slice(start, start + width)
        start += width
        sums = []
        for p, matrix in enumerate((gate_matrix, up_matrix)):
            delta = (low_rank_scale * dot(spread[p], expand[:, cut])).astype(bf16)
            sums.append(dot(mixed, matrix[:, cut]) + delta.astype(f32))
        both = jnp.stack(sums)
        own = both[:, :half] + core_swap(both[:, half:].astype(bf16), replicas).astype(f32)
        if GATHERED:
            away = own.astype(bf16)
            own = own[:, :block]
            for step in range(1, chips):
                own = own + from_chip(
                    away[:, step * block : (step + 1) * block], replicas, chips - step
                ).astype(f32)
        else:
            away = own.astype(bf16)
            for step in range(1, chips):
                got = from_chip(away, replicas, step).astype(f32)
                got = jnp.roll(got, step * block, axis=1) if chips > 2 else jnp.concatenate(
                    [got[:, block:], got[:, :block]], axis=1
                )
                own = own + got
        hidden = (jax.nn.silu(own[0]) * own[1]).astype(bf16)
        if GATHERED:
            hidden = jnp.concatenate(
                [hidden] + [from_chip(hidden, replicas, step) for step in range(1, chips)], axis=0
            )
        hidden = jnp.concatenate([hidden, core_swap(hidden, replicas)], axis=0)
        part = dot(hidden, down_weight[cut])
        total = part if total is None else total + part

    share = rows // depth
    blocks = total.reshape(depth, share, -1)
    pick = [lax.dynamic_index_in_dim(blocks, (layer + s) % depth, 0, False) for s in range(depth)]
    mine = pick[0]
    for s in range(1, depth):
        pairs = [(i, (i + s) % depth) for i in range(depth)]
        mine = mine + lax.ppermute(pick[s].astype(bf16), "tensor", pairs).astype(f32)
    mine = mine.astype(bf16)
    got = [mine]
    for s in range(1, depth):
        pairs = [((i + s) % depth, i) for i in range(depth)]
        got.append(lax.ppermute(mine, "tensor", pairs))
    held = (layer + place // share) % depth * share + place % share
    gather = (held[:, None] == place[None, :]).astype(bf16)
    back = dot(order.T, gather.T).astype(bf16)
    return dot(back, jnp.concatenate(got, axis=0)).astype(bf16)


def solution(mesh):
    placed = (
        P("groups", "replica"),
        P("replica", "tensor"),
        P("replica", "tensor"),
        P("tensor", "replica"),
        P("replica", None, None, None),
        P("replica", None, None, "tensor"),
        P("groups"),
        P("groups"),
    )
    return jax.shard_map(
        shards, mesh=mesh, in_specs=placed, out_specs=P("groups", "replica"), check_vma=False
    )
```

```python
import functools

import jax
import jax.numpy as jnp
from jax import lax
from jax.experimental import pallas as pl
from jax.experimental.pallas import tpu as pltpu
from jax.sharding import PartitionSpec as P

low_rank_scale = 0.5
f32 = jnp.float32
bf16 = jnp.bfloat16
MIB = 1 << 20
CHUNKS = (1280, 1280, 1280, 1280, 1280)
TILE = 640


def dot(a, b):
    return jnp.dot(a, b, preferred_element_type=f32)


def core_swap(value, replicas):
    return lax.ppermute(value, "replica", [(i, i ^ 1) for i in range(replicas)])


def from_chip(value, replicas, step, flip=0):
    pairs = [((i + 2 * step) % replicas ^ flip, i) for i in range(replicas)]
    return lax.ppermute(value, "replica", pairs)


def row_order(rows, block, chips, me, transposed=False):
    mine = lax.broadcasted_iota(jnp.int32, (rows, rows), 1 if transposed else 0)
    batch = lax.broadcasted_iota(jnp.int32, (rows, rows), 0 if transposed else 1)
    nth = mine // block
    chip = (me // 2 + nth % chips) % chips
    core = (me % 2 + nth // chips) % 2
    return (batch == (chip * 2 + core) * block + mine % block).astype(f32).astype(bf16)


def widen_into(spread, expand_ref, base_ref, start, width, own_ref, away_ref):
    half = own_ref.shape[1]
    rows = 2 * half
    delta = dot(spread, expand_ref[:, start : start + width])
    delta = (low_rank_scale * delta).astype(bf16).astype(f32)
    for p in range(2):
        total = base_ref[p, :, start : start + width] + delta[p * rows : (p + 1) * rows]
        own_ref[p] = total[:half]
        away_ref[p] = total[half:].astype(bf16)


def shrink_kernel(block, sources, ids_ref, slots_ref, down_ref, expand_ref, base_ref, *refs):
    pieces, (spread_ref, own_ref, away_ref) = refs[:-3], refs[-3:]
    me = lax.axis_index("replica")
    rows, width = pieces[0].shape
    stored, _, rank, _ = down_ref.shape
    table = stored * 2 * rank
    total = jnp.zeros((rows, table), f32)
    for piece, source in zip(pieces, sources(me)):
        columns = pl.ds(pl.multiple_of(source * width, 128), width)
        part = down_ref[:, :, :, columns].reshape(table, width)
        total += lax.dot_general(piece[...], part, (((1,), (1,)), ((), ())), preferred_element_type=f32)
    shrink = total.astype(bf16).astype(f32)
    adapters = slots_ref.shape[1]
    known = lax.broadcasted_iota(jnp.int32, (adapters, rows), 0)
    chosen = (known == ids_ref[...]).astype(f32).astype(bf16)
    slots = jnp.broadcast_to(slots_ref[...].astype(f32), (table, adapters)).astype(bf16)
    slot = lax.dot_general(chosen, slots, (((0,), (1,)), ((), ())), preferred_element_type=f32)
    first = (slot.astype(jnp.int32) - me * stored) * (2 * rank)
    column = lax.broadcasted_iota(jnp.int32, (rows, table), 1)
    order = row_order(rows, block, len(pieces) // 2, me)
    for p in range(2):
        begin = first + p * rank
        mine = jnp.logical_and(column >= begin, column < begin + rank)
        picked = jnp.where(mine, shrink, 0.0).astype(bf16)
        spread_ref[p * rows : (p + 1) * rows] = dot(order, picked).astype(bf16)
    widen_into(spread_ref[...], expand_ref, base_ref, 0, own_ref.shape[2], own_ref, away_ref)


def parted(half, width):
    return [jax.ShapeDtypeStruct((2, half, width), f32), jax.ShapeDtypeStruct((2, half, width), bf16)]


def shrink_rows(pieces, sources, block, ids, slots, adapter_down, expand, base, width):
    rows = ids.shape[0]
    vmem = pl.BlockSpec(memory_space=pltpu.VMEM)
    return pl.pallas_call(
        functools.partial(shrink_kernel, block, sources),
        out_shape=[jax.ShapeDtypeStruct((2 * rows, expand.shape[0]), bf16)] + parted(rows // 2, width),
        in_specs=[vmem] * (5 + len(pieces)),
        out_specs=[vmem] * 3,
        compiler_params=pltpu.CompilerParams(vmem_limit_bytes=(16 if rows <= 64 else 40) * MIB),
        cost_estimate=pl.CostEstimate(
            flops=2 * adapter_down.size * rows, bytes_accessed=2 * adapter_down.size, transcendentals=0
        ),
        name="shrink",
    )(ids.reshape(1, rows), slots.reshape(1, -1), adapter_down, expand, base, *pieces)


def widen_kernel(widths, start, spread_ref, expand_ref, base_ref, *out_refs):
    for k, width in enumerate(widths):
        widen_into(spread_ref[...], expand_ref, base_ref, start, width, out_refs[2 * k], out_refs[2 * k + 1])
        start += width


def widen(spread, expand, base, start, widths):
    half = spread.shape[0] // 4
    vmem = pl.BlockSpec(memory_space=pltpu.VMEM)
    return pl.pallas_call(
        functools.partial(widen_kernel, widths, start),
        out_shape=[shape for width in widths for shape in parted(half, width)],
        in_specs=[vmem] * 3,
        out_specs=[vmem] * (2 * len(widths)),
        compiler_params=pltpu.CompilerParams(vmem_limit_bytes=16 * MIB),
        cost_estimate=pl.CostEstimate(
            flops=2 * spread.size * sum(widths), bytes_accessed=4 * spread.size, transcendentals=0
        ),
        name="widen",
    )(spread, expand, base)


def stream_kernel(block, chips, tile, x_ref, gate_ref, up_ref, out_ref, mixed, held, arrived):
    slots = held.shape[0]
    rows = x_ref.shape[0]
    work = [(p, at) for at in range(0, gate_ref.shape[1], tile) for p in range(2)]

    def fetch(i):
        p, at = work[i]
        source = (gate_ref, up_ref)[p].at[:, pl.ds(at, tile)]
        return pltpu.make_async_copy(source, held.at[i % slots], arrived.at[i % slots])

    for i in range(min(slots, len(work))):
        fetch(i).start()
    order = row_order(rows, block, chips, lax.axis_index("replica"))
    mixed[...] = dot(order, x_ref[...]).astype(bf16)
    for i, (p, at) in enumerate(work):
        fetch(i).wait()
        out_ref[p, :, at : at + tile] = dot(mixed[...], held[i % slots])
        if i + slots < len(work):
            fetch(i + slots).start()


def stream(x, gate, up, block, chips, tile, slots=8):
    rows, depth = x.shape
    width = gate.shape[1]
    vmem = pl.BlockSpec(memory_space=pltpu.VMEM)
    far = pl.BlockSpec(memory_space=pltpu.HBM)
    return pl.pallas_call(
        functools.partial(stream_kernel, block, chips, tile),
        out_shape=jax.ShapeDtypeStruct((2, rows, width), f32),
        in_specs=[vmem, far, far],
        out_specs=vmem,
        scratch_shapes=[
            pltpu.VMEM((rows, depth), bf16),
            pltpu.VMEM((slots, depth, tile), bf16),
            pltpu.SemaphoreType.DMA((slots,)),
        ],
        compiler_params=pltpu.CompilerParams(vmem_limit_bytes=50 * MIB),
        cost_estimate=pl.CostEstimate(
            flops=4 * rows * depth * width, bytes_accessed=4 * depth * width, transcendentals=0
        ),
        name="stream",
    )(x, gate, up)


def join_kernel(own_ref, got_ref, sum_ref, send_ref):
    total = own_ref[...] + got_ref[...].astype(f32)
    sum_ref[...] = total
    send_ref[...] = total.astype(bf16)


def join(own, got):
    vmem = pl.BlockSpec(memory_space=pltpu.VMEM)
    return pl.pallas_call(
        join_kernel,
        out_shape=[jax.ShapeDtypeStruct(own.shape, f32), jax.ShapeDtypeStruct(own.shape, bf16)],
        in_specs=[vmem] * 2,
        out_specs=[vmem] * 2,
        compiler_params=pltpu.CompilerParams(vmem_limit_bytes=8 * MIB),
        cost_estimate=pl.CostEstimate(flops=1, bytes_accessed=1, transcendentals=0),
        name="join",
    )(own, got)


def activate_kernel(block, own_ref, *refs):
    hidden_ref = refs[-1]
    half = own_ref.shape[1]

    def total(p, lo):
        sums = own_ref[p, lo : lo + block]
        for step, got_ref in enumerate(refs[:-1], 1):
            at = (lo - step * block) % half
            sums += got_ref[p, at : at + block].astype(f32)
        return sums

    for lo in range(0, half, block):
        gate, up = total(0, lo), total(1, lo)
        hidden_ref[lo : lo + block] = (gate / (1.0 + jnp.exp(-gate)) * up).astype(bf16)


def activate(block, own, gots):
    vmem = pl.BlockSpec(memory_space=pltpu.VMEM)
    return pl.pallas_call(
        functools.partial(activate_kernel, block),
        out_shape=jax.ShapeDtypeStruct(own.shape[1:], bf16),
        in_specs=[vmem] * (1 + len(gots)),
        out_specs=vmem,
        compiler_params=pltpu.CompilerParams(vmem_limit_bytes=8 * MIB),
        cost_estimate=pl.CostEstimate(flops=1, bytes_accessed=1, transcendentals=0),
        name="activate",
    )(own, *gots)


def project_kernel(start, own_ref, got_ref, down_ref, *refs):
    total_ref, hidden, held, arrived = refs[-4:]
    half = own_ref.shape[0]
    pieces, depth, _ = held.shape

    def fetch(i):
        source = down_ref.at[pl.ds(start + i * depth, depth)]
        return pltpu.make_async_copy(source, held.at[i], arrived.at[i])

    for i in range(pieces):
        fetch(i).start()
    hidden[:half] = own_ref[...]
    hidden[half:] = got_ref[...]
    total = refs[0][...] if len(refs) > 4 else jnp.zeros(total_ref.shape, f32)
    for i in range(pieces):
        fetch(i).wait()
        total += dot(hidden[:, i * depth : (i + 1) * depth], held[i])
    total_ref[...] = total


def project(start, own, got, down, total, depth=256):
    half, width = own.shape
    depth = depth if width % depth == 0 else 128
    rows, columns = 2 * half, down.shape[1]
    vmem = pl.BlockSpec(memory_space=pltpu.VMEM)
    before = [] if total is None else [total]
    return pl.pallas_call(
        functools.partial(project_kernel, start),
        out_shape=jax.ShapeDtypeStruct((rows, columns), f32),
        in_specs=[vmem] * 2 + [pl.BlockSpec(memory_space=pltpu.HBM)] + [vmem] * len(before),
        out_specs=vmem,
        scratch_shapes=[
            pltpu.VMEM((rows, width), bf16),
            pltpu.VMEM((width // depth, depth, columns), bf16),
            pltpu.SemaphoreType.DMA((width // depth,)),
        ],
        compiler_params=pltpu.CompilerParams(vmem_limit_bytes=50 * MIB),
        cost_estimate=pl.CostEstimate(flops=1, bytes_accessed=1, transcendentals=0),
        name="project",
    )(own, got, down, *before)


def shards(
    tokens, gate_matrix, up_matrix, down_weight, adapter_down, adapter_up, adapter_ids, adapter_slot
):
    replicas, depth = lax.axis_size("replica"), lax.axis_size("tensor")
    chips = replicas // 2
    layer = lax.axis_index("tensor")
    rows = tokens.shape[0]
    block = rows // replicas
    half = rows // 2
    units = gate_matrix.shape[1]

    pieces = [tokens, core_swap(tokens, replicas)]
    for step in range(1, chips):
        for flip in range(2):
            pieces.append(from_chip(tokens, replicas, step, flip))

    def sources(me):
        far = [((me + 2 * step) % replicas, flip) for step in range(1, chips) for flip in range(2)]
        near = [(me, 0), (me, 1)]
        return [at + flip * (1 - 2 * (at % 2)) for at, flip in near + far]

    widths = CHUNKS if sum(CHUNKS) == units else (units,)
    base = stream(tokens, gate_matrix, up_matrix, block, chips, TILE)
    expand = adapter_up.reshape(-1, units)
    spread, own, away = shrink_rows(
        pieces, sources, block, adapter_ids, adapter_slot, adapter_down, expand, base, widths[0]
    )
    parts = [own, away]
    if len(widths) > 1:
        parts += widen(spread, expand, base, widths[0], widths[1:])
    swapped = [core_swap(away, replicas) for away in parts[1::2]]
    joined = [join(own, got) for own, got in zip(parts[::2], swapped)]
    gots = [[from_chip(away, replicas, step) for step in range(1, chips)] for _, away in joined]
    total = None
    start = 0
    for width, (own, _), got in zip(widths, joined, gots):
        if total is not None:
            total, *got = lax.optimization_barrier((total, *got))
        hidden = activate(block, own, got)
        total = project(start, hidden, core_swap(hidden, replicas), down_weight, total)
        start += width

    share = rows // depth
    blocks = total.reshape(depth, share, -1)
    pick = [lax.dynamic_index_in_dim(blocks, (layer + s) % depth, 0, False) for s in range(depth)]
    mine = pick[0]
    for s in range(1, depth):
        pairs = [(i, (i + s) % depth) for i in range(depth)]
        mine = mine + lax.ppermute(pick[s].astype(bf16), "tensor", pairs).astype(f32)
    mine = mine.astype(bf16)
    got = [mine]
    for s in range(1, depth):
        pairs = [((i + s) % depth, i) for i in range(depth)]
        got.append(lax.ppermute(mine, "tensor", pairs))
    place = jnp.arange(rows, dtype=jnp.int32)
    held = (layer + place // share) % depth * share + place % share
    gather = (held[:, None] == place[None, :]).astype(bf16)
    order = row_order(rows, block, chips, lax.axis_index("replica"), True)
    back = dot(order, gather.T).astype(bf16)
    return dot(back, jnp.concatenate(got, axis=0)).astype(bf16)


def solution(mesh):
    placed = (
        P("groups", "replica"),
        P("replica", "tensor"),
        P("replica", "tensor"),
        P("tensor", "replica"),
        P("replica", None, None, None),
        P("replica", None, None, "tensor"),
        P("groups"),
        P("groups"),
    )
    return jax.shard_map(
        shards, mesh=mesh, in_specs=placed, out_specs=P("groups", "replica"), check_vma=False
    )
```

```python
import functools

import jax
import jax.numpy as jnp
from jax import lax
from jax.experimental import pallas as pl
from jax.experimental.pallas import tpu as pltpu
from jax.sharding import PartitionSpec as P

low_rank_scale = 0.5
f32 = jnp.float32
bf16 = jnp.bfloat16
MIB = 1 << 20
CHUNKS = (2560, 2560, 1280)
PIECE = 256


def dot(a, b):
    return jnp.dot(a, b, preferred_element_type=f32)


def core_swap(value, replicas):
    return lax.ppermute(value, "replica", [(i, i ^ 1) for i in range(replicas)])


def from_chip(value, replicas, step, flip=0):
    pairs = [((i + 2 * step) % replicas ^ flip, i) for i in range(replicas)]
    return lax.ppermute(value, "replica", pairs)


def row_order(rows, block, chips, me):
    mine = lax.broadcasted_iota(jnp.int32, (rows, rows), 0)
    batch = lax.broadcasted_iota(jnp.int32, (rows, rows), 1)
    nth = mine // block
    chip = (me // 2 + nth % chips) % chips
    core = (me % 2 + nth // chips) % 2
    return (batch == (chip * 2 + core) * block + mine % block).astype(f32).astype(bf16)


def widen_into(spread, expand_ref, base_ref, at, start, own_ref, away_ref):
    _, half, width = own_ref.shape
    rows = 2 * half
    delta = dot(spread, expand_ref[:, start : start + width])
    delta = (low_rank_scale * delta).astype(bf16).astype(f32)
    for p in range(2):
        total = base_ref[p, :, at : at + width] + delta[p * rows : (p + 1) * rows]
        own_ref[p] = total[:half]
        away_ref[p] = total[half:].astype(bf16)


def shrink_kernel(block, sources, ids_ref, slots_ref, down_ref, expand_ref, base_ref, *refs):
    pieces, (spread_ref, own_ref, away_ref) = refs[:-3], refs[-3:]
    me = lax.axis_index("replica")
    rows, width = pieces[0].shape
    stored, _, rank, _ = down_ref.shape
    table = stored * 2 * rank
    total = jnp.zeros((rows, table), f32)
    for piece, source in zip(pieces, sources(me)):
        columns = pl.ds(pl.multiple_of(source * width, 128), width)
        part = down_ref[:, :, :, columns].reshape(table, width)
        total += lax.dot_general(piece[...], part, (((1,), (1,)), ((), ())), preferred_element_type=f32)
    shrink = total.astype(bf16).astype(f32)
    adapters = slots_ref.shape[1]
    known = lax.broadcasted_iota(jnp.int32, (adapters, rows), 0)
    chosen = (known == ids_ref[...]).astype(f32).astype(bf16)
    slots = jnp.broadcast_to(slots_ref[...].astype(f32), (table, adapters)).astype(bf16)
    slot = lax.dot_general(chosen, slots, (((0,), (1,)), ((), ())), preferred_element_type=f32)
    first = (slot.astype(jnp.int32) - me * stored) * (2 * rank)
    column = lax.broadcasted_iota(jnp.int32, (rows, table), 1)
    order = row_order(rows, block, len(pieces) // 2, me)
    for p in range(2):
        begin = first + p * rank
        mine = jnp.logical_and(column >= begin, column < begin + rank)
        picked = jnp.where(mine, shrink, 0.0).astype(bf16)
        spread_ref[p * rows : (p + 1) * rows] = dot(order, picked).astype(bf16)
    widen_into(spread_ref[...], expand_ref, base_ref, 0, 0, own_ref, away_ref)


def parted(half, width):
    return [jax.ShapeDtypeStruct((2, half, width), f32), jax.ShapeDtypeStruct((2, half, width), bf16)]


def shrink_rows(pieces, sources, block, ids, slots, adapter_down, expand, base, width):
    rows = ids.shape[0]
    vmem = pl.BlockSpec(memory_space=pltpu.VMEM)
    return pl.pallas_call(
        functools.partial(shrink_kernel, block, sources),
        out_shape=[jax.ShapeDtypeStruct((2 * rows, expand.shape[0]), bf16)] + parted(rows // 2, width),
        in_specs=[vmem] * (5 + len(pieces)),
        out_specs=[vmem] * 3,
        compiler_params=pltpu.CompilerParams(vmem_limit_bytes=(16 if rows <= 64 else 40) * MIB),
        cost_estimate=pl.CostEstimate(
            flops=2 * adapter_down.size * rows, bytes_accessed=2 * adapter_down.size, transcendentals=0
        ),
        name="shrink",
    )(ids.reshape(1, rows), slots.reshape(1, -1), adapter_down, expand, base, *pieces)


def widen_kernel(widths, at, start, spread_ref, expand_ref, base_ref, *out_refs):
    for k, width in enumerate(widths):
        widen_into(spread_ref[...], expand_ref, base_ref, at, start, out_refs[2 * k], out_refs[2 * k + 1])
        at += width
        start += width


def widen(spread, expand, base, at, start, widths):
    half = spread.shape[0] // 4
    vmem = pl.BlockSpec(memory_space=pltpu.VMEM)
    return pl.pallas_call(
        functools.partial(widen_kernel, widths, at, start),
        out_shape=[shape for width in widths for shape in parted(half, width)],
        in_specs=[vmem] * 3,
        out_specs=[vmem] * (2 * len(widths)),
        compiler_params=pltpu.CompilerParams(vmem_limit_bytes=16 * MIB),
        cost_estimate=pl.CostEstimate(
            flops=2 * spread.size * sum(widths), bytes_accessed=4 * spread.size, transcendentals=0
        ),
        name="widen",
    )(spread, expand, base)


def stream_kernel(block, chips, start, tile, x_ref, gate_ref, up_ref, out_ref, rows_in, mixed, held, arrived):
    slots = held.shape[0]
    rows = x_ref.shape[0]
    work = [(p, at) for at in range(0, out_ref.shape[2], tile) for p in range(2)]

    def fetch(i):
        p, at = work[i]
        source = (gate_ref, up_ref)[p].at[:, pl.ds(start + at, tile)]
        return pltpu.make_async_copy(source, held.at[i % slots], arrived.at[i % slots])

    enter = pltpu.make_async_copy(x_ref, rows_in, arrived.at[slots])
    enter.start()
    for i in range(min(slots, len(work))):
        fetch(i).start()
    order = row_order(rows, block, chips, lax.axis_index("replica"))
    enter.wait()
    mixed[...] = dot(order, rows_in[...]).astype(bf16)
    for i, (p, at) in enumerate(work):
        fetch(i).wait()
        out_ref[p, :, at : at + tile] = dot(mixed[...], held[i % slots])
        if i + slots < len(work):
            fetch(i + slots).start()


def stream(x, gate, up, block, chips, start, width, slots=8):
    rows, depth = x.shape
    tile = max(t for t in range(128, 641, 128) if width % t == 0)
    far = pl.BlockSpec(memory_space=pltpu.HBM)
    return pl.pallas_call(
        functools.partial(stream_kernel, block, chips, start, tile),
        out_shape=jax.ShapeDtypeStruct((2, rows, width), f32),
        in_specs=[far] * 3,
        out_specs=pl.BlockSpec(memory_space=pltpu.VMEM),
        scratch_shapes=[
            pltpu.VMEM((rows, depth), bf16),
            pltpu.VMEM((rows, depth), bf16),
            pltpu.VMEM((slots, depth, tile), bf16),
            pltpu.SemaphoreType.DMA((slots + 1,)),
        ],
        compiler_params=pltpu.CompilerParams(vmem_limit_bytes=50 * MIB),
        cost_estimate=pl.CostEstimate(
            flops=4 * rows * depth * width, bytes_accessed=4 * depth * width, transcendentals=0
        ),
        name="stream",
    )(x, gate, up)


def join_kernel(own_ref, got_ref, sum_ref, *send_refs):
    block = sum_ref.shape[1]
    total = own_ref[...] + got_ref[...].astype(f32)
    sum_ref[...] = total[:, :block]
    for step, send_ref in enumerate(send_refs, 1):
        send_ref[...] = total[:, step * block : (step + 1) * block].astype(bf16)


def join(block, own, got):
    vmem = pl.BlockSpec(memory_space=pltpu.VMEM)
    _, half, width = own.shape
    away = half // block - 1
    return pl.pallas_call(
        join_kernel,
        out_shape=[jax.ShapeDtypeStruct((2, block, width), f32)]
        + [jax.ShapeDtypeStruct((2, block, width), bf16)] * away,
        in_specs=[vmem] * 2,
        out_specs=[vmem] * (1 + away),
        compiler_params=pltpu.CompilerParams(vmem_limit_bytes=8 * MIB),
        cost_estimate=pl.CostEstimate(flops=1, bytes_accessed=1, transcendentals=0),
        name="join",
    )(own, got)


def activate_kernel(own_ref, *refs):
    def total(p):
        sums = own_ref[p]
        for got_ref in refs[:-1]:
            sums += got_ref[p].astype(f32)
        return sums

    gate, up = total(0), total(1)
    refs[-1][...] = (gate / (1.0 + jnp.exp(-gate)) * up).astype(bf16)


def activate(own, gots):
    vmem = pl.BlockSpec(memory_space=pltpu.VMEM)
    return pl.pallas_call(
        activate_kernel,
        out_shape=jax.ShapeDtypeStruct(own.shape[1:], bf16),
        in_specs=[vmem] * (1 + len(gots)),
        out_specs=vmem,
        compiler_params=pltpu.CompilerParams(vmem_limit_bytes=8 * MIB),
        cost_estimate=pl.CostEstimate(flops=1, bytes_accessed=1, transcendentals=0),
        name="activate",
    )(own, *gots)


def fetch_kernel(down_ref, after_ref, out_ref, arrived):
    copy = pltpu.make_async_copy(down_ref.at[pl.ds(0, out_ref.shape[0])], out_ref, arrived)
    copy.start()
    copy.wait()


def fetch(down, after, rows):
    far = pl.BlockSpec(memory_space=pltpu.HBM)
    return pl.pallas_call(
        fetch_kernel,
        out_shape=jax.ShapeDtypeStruct((rows, down.shape[1]), bf16),
        in_specs=[far, pl.BlockSpec(memory_space=pl.ANY)],
        out_specs=pl.BlockSpec(memory_space=pltpu.VMEM),
        scratch_shapes=[pltpu.SemaphoreType.DMA(())],
        compiler_params=pltpu.CompilerParams(vmem_limit_bytes=40 * MIB),
        cost_estimate=pl.CostEstimate(flops=1, bytes_accessed=1, transcendentals=0),
        name="fetch",
    )(down, after)


def project_kernel(count, near_ref, down_ref, *refs):
    blocks, (total_ref, hidden, held, arrived) = refs[:-4], refs[-4:]
    pieces, depth, columns = held.shape
    near = near_ref.shape[0]

    def bring(i):
        source = down_ref.at[pl.ds(near + i * depth, depth)]
        return pltpu.make_async_copy(source, held.at[i], arrived.at[i])

    for i in range(pieces):
        bring(i).start()
    me = lax.axis_index("replica")
    chips = count // 2
    start = 0
    for c in range(len(blocks) // count):
        parts = blocks[c * count : (c + 1) * count]
        block, width = parts[0].shape
        for nth, ref in enumerate(parts):
            chip = (me // 2 + nth % chips) % chips
            at = (chip * 2 + (me + nth // chips) % 2) * block
            hidden[pl.ds(pl.multiple_of(at, 16), block), start : start + width] = ref[...]
        start += width
    total = dot(hidden[:, :near], near_ref[...])
    for i in range(pieces):
        bring(i).wait()
        total += dot(hidden[:, near + i * depth : near + (i + 1) * depth], held[i])
    total_ref[...] = total.astype(bf16)


def project(chunks, near, down):
    count = len(chunks[0])
    rows = count * chunks[0][0].shape[0]
    vmem = pl.BlockSpec(memory_space=pltpu.VMEM)
    far = pl.BlockSpec(memory_space=pltpu.HBM)
    blocks = [value for chunk in chunks for value in chunk]
    pieces = (down.shape[0] - near.shape[0]) // PIECE
    return pl.pallas_call(
        functools.partial(project_kernel, count),
        out_shape=jax.ShapeDtypeStruct((rows, down.shape[1]), bf16),
        in_specs=[vmem, far] + [vmem] * len(blocks),
        out_specs=vmem,
        scratch_shapes=[
            pltpu.VMEM((rows, down.shape[0]), bf16),
            pltpu.VMEM((pieces, PIECE, down.shape[1]), bf16),
            pltpu.SemaphoreType.DMA((pieces,)),
        ],
        compiler_params=pltpu.CompilerParams(vmem_limit_bytes=40 * MIB),
        cost_estimate=pl.CostEstimate(
            flops=2 * rows * down.size, bytes_accessed=2 * down.size, transcendentals=0
        ),
        name="project",
    )(near, down, *blocks)


def shards(
    tokens, gate_matrix, up_matrix, down_weight, adapter_down, adapter_up, adapter_ids, adapter_slot
):
    replicas, depth = lax.axis_size("replica"), lax.axis_size("tensor")
    chips = replicas // 2
    rows = tokens.shape[0]
    block = rows // replicas
    half = rows // 2
    units = gate_matrix.shape[1]

    pieces = [tokens, core_swap(tokens, replicas)]
    for step in range(1, chips):
        for flip in range(2):
            pieces.append(from_chip(tokens, replicas, step, flip))

    def sources(me):
        far = [((me + 2 * step) % replicas, flip) for step in range(1, chips) for flip in range(2)]
        near = [(me, 0), (me, 1)]
        return [at + flip * (1 - 2 * (at % 2)) for at, flip in near + far]

    widths = CHUNKS if sum(CHUNKS) == units else (units,)
    base = stream(tokens, gate_matrix, up_matrix, block, chips, 0, units)
    expand = adapter_up.reshape(-1, units)
    spread, *parts = shrink_rows(
        pieces, sources, block, adapter_ids, adapter_slot, adapter_down, expand, base, widths[0]
    )
    if len(widths) > 1:
        parts += widen(spread, expand, base, widths[0], widths[0], widths[1:])
    sums = []
    for own, away in zip(parts[::2], parts[1::2]):
        own, *sends = join(block, own, core_swap(away, replicas))
        gots = [from_chip(send, replicas, chips - step) for step, send in enumerate(sends, 1)]
        sums.append((own, gots))
    chunks = []
    near = fetch(down_weight, sums[-1][0], units * 3 // 5)
    own, gots = sums[0]
    near, *gots = lax.optimization_barrier((near, *gots))
    sums[0] = own, gots
    for own, gots in sums:
        hidden = activate(own, gots)
        blocks = [hidden] + [from_chip(hidden, replicas, step) for step in range(1, chips)]
        chunks.append(blocks + [core_swap(value, replicas) for value in blocks])
    total = project(chunks, near, down_weight)
    reach = 1
    while reach < depth:
        pairs = [(i, i ^ (2 * reach - 1)) for i in range(depth)]
        total = (total.astype(f32) + lax.ppermute(total, "tensor", pairs).astype(f32)).astype(bf16)
        reach *= 2
    return total


def solution(mesh):
    placed = (
        P("groups", "replica"),
        P("replica", "tensor"),
        P("replica", "tensor"),
        P("tensor", "replica"),
        P("replica", None, None, None),
        P("replica", None, None, "tensor"),
        P("groups"),
        P("groups"),
    )
    return jax.shard_map(
        shards, mesh=mesh, in_specs=placed, out_specs=P("groups", "replica"), check_vma=False
    )
```

```python
import functools

import jax
import jax.numpy as jnp
from jax import lax
from jax.experimental import pallas as pl
from jax.experimental.pallas import tpu as pltpu
from jax.sharding import PartitionSpec as P

low_rank_scale = 0.5
f32 = jnp.float32
bf16 = jnp.bfloat16
MIB = 1 << 20
CHUNKS = (2560, 2560, 1280)
PIECE = 512
TILE = 256


def dot(a, b):
    return jnp.dot(a, b, preferred_element_type=f32)


def core_swap(value, replicas):
    return lax.ppermute(value, "replica", [(i, i ^ 1) for i in range(replicas)])


def from_chip(value, replicas, step, flip=0):
    pairs = [((i + 2 * step) % replicas ^ flip, i) for i in range(replicas)]
    return lax.ppermute(value, "replica", pairs)


def row_order(rows, block, chips, me):
    mine = lax.broadcasted_iota(jnp.int32, (rows, rows), 0)
    batch = lax.broadcasted_iota(jnp.int32, (rows, rows), 1)
    nth = mine // block
    chip = (me // 2 + nth % chips) % chips
    core = (me % 2 + nth // chips) % 2
    return (batch == (chip * 2 + core) * block + mine % block).astype(f32).astype(bf16)


def widen_into(spread, expand_ref, base_ref, at, start, own_ref, away_ref):
    _, half, width = own_ref.shape
    rows = 2 * half
    delta = dot(spread, expand_ref[:, start : start + width])
    delta = (low_rank_scale * delta).astype(bf16).astype(f32)
    for p in range(2):
        total = base_ref[p, :, at : at + width] + delta[p * rows : (p + 1) * rows]
        own_ref[p] = total[:half]
        away_ref[p] = total[half:].astype(bf16)


def shrink_kernel(block, sources, ids_ref, slots_ref, down_ref, expand_ref, base_ref, *refs):
    pieces, (spread_ref, own_ref, away_ref) = refs[:-3], refs[-3:]
    me = lax.axis_index("replica")
    rows, width = pieces[0].shape
    stored, _, rank, _ = down_ref.shape
    table = stored * 2 * rank
    total = jnp.zeros((rows, table), f32)
    for piece, source in zip(pieces, sources(me)):
        columns = pl.ds(pl.multiple_of(source * width, 128), width)
        part = down_ref[:, :, :, columns].reshape(table, width)
        total += lax.dot_general(piece[...], part, (((1,), (1,)), ((), ())), preferred_element_type=f32)
    shrink = total.astype(bf16).astype(f32)
    adapters = slots_ref.shape[1]
    known = lax.broadcasted_iota(jnp.int32, (adapters, rows), 0)
    chosen = (known == ids_ref[...]).astype(f32).astype(bf16)
    slots = jnp.broadcast_to(slots_ref[...].astype(f32), (table, adapters)).astype(bf16)
    slot = lax.dot_general(chosen, slots, (((0,), (1,)), ((), ())), preferred_element_type=f32)
    first = (slot.astype(jnp.int32) - me * stored) * (2 * rank)
    column = lax.broadcasted_iota(jnp.int32, (rows, table), 1)
    order = row_order(rows, block, len(pieces) // 2, me)
    for p in range(2):
        begin = first + p * rank
        mine = jnp.logical_and(column >= begin, column < begin + rank)
        picked = jnp.where(mine, shrink, 0.0).astype(bf16)
        spread_ref[p * rows : (p + 1) * rows] = dot(order, picked).astype(bf16)
    widen_into(spread_ref[...], expand_ref, base_ref, 0, 0, own_ref, away_ref)


def parted(half, width):
    return [jax.ShapeDtypeStruct((2, half, width), f32), jax.ShapeDtypeStruct((2, half, width), bf16)]


def shrink_rows(pieces, sources, block, ids, slots, adapter_down, expand, base, width):
    rows = ids.shape[0]
    vmem = pl.BlockSpec(memory_space=pltpu.VMEM)
    return pl.pallas_call(
        functools.partial(shrink_kernel, block, sources),
        out_shape=[jax.ShapeDtypeStruct((2 * rows, expand.shape[0]), bf16)] + parted(rows // 2, width),
        in_specs=[vmem] * (5 + len(pieces)),
        out_specs=[vmem] * 3,
        compiler_params=pltpu.CompilerParams(vmem_limit_bytes=(16 if rows <= 64 else 40) * MIB),
        cost_estimate=pl.CostEstimate(
            flops=2 * adapter_down.size * rows, bytes_accessed=2 * adapter_down.size, transcendentals=0
        ),
        name="shrink",
    )(ids.reshape(1, rows), slots.reshape(1, -1), adapter_down, expand, base, *pieces)


def widen_kernel(widths, at, start, spread_ref, expand_ref, base_ref, *out_refs):
    for k, width in enumerate(widths):
        widen_into(spread_ref[...], expand_ref, base_ref, at, start, out_refs[2 * k], out_refs[2 * k + 1])
        at += width
        start += width


def widen(spread, expand, base, at, start, widths):
    half = spread.shape[0] // 4
    vmem = pl.BlockSpec(memory_space=pltpu.VMEM)
    return pl.pallas_call(
        functools.partial(widen_kernel, widths, at, start),
        out_shape=[shape for width in widths for shape in parted(half, width)],
        in_specs=[vmem] * 3,
        out_specs=[vmem] * (2 * len(widths)),
        compiler_params=pltpu.CompilerParams(vmem_limit_bytes=16 * MIB),
        cost_estimate=pl.CostEstimate(
            flops=2 * spread.size * sum(widths), bytes_accessed=4 * spread.size, transcendentals=0
        ),
        name="widen",
    )(spread, expand, base)


def stream_kernel(block, chips, start, tile, x_ref, gate_ref, up_ref, out_ref, rows_in, mixed, held, arrived):
    slots = held.shape[0]
    rows = x_ref.shape[0]
    work = [(p, at) for at in range(0, out_ref.shape[2], tile) for p in range(2)]

    def fetch(i):
        p, at = work[i]
        source = (gate_ref, up_ref)[p].at[:, pl.ds(start + at, tile)]
        return pltpu.make_async_copy(source, held.at[i % slots], arrived.at[i % slots])

    enter = pltpu.make_async_copy(x_ref, rows_in, arrived.at[slots])
    enter.start()
    for i in range(min(slots, len(work))):
        fetch(i).start()
    order = row_order(rows, block, chips, lax.axis_index("replica"))
    enter.wait()
    mixed[...] = dot(order, rows_in[...]).astype(bf16)
    for i, (p, at) in enumerate(work):
        fetch(i).wait()
        out_ref[p, :, at : at + tile] = dot(mixed[...], held[i % slots])
        if i + slots < len(work):
            fetch(i + slots).start()


def stream(x, gate, up, block, chips, start, width, slots=8):
    rows, depth = x.shape
    tile = max(t for t in range(128, 641, 128) if width % t == 0)
    far = pl.BlockSpec(memory_space=pltpu.HBM)
    return pl.pallas_call(
        functools.partial(stream_kernel, block, chips, start, tile),
        out_shape=[jax.ShapeDtypeStruct((2, rows, width), f32), jax.ShapeDtypeStruct(x.shape, bf16)],
        in_specs=[far] * 3,
        out_specs=[pl.BlockSpec(memory_space=pltpu.VMEM)] * 2,
        scratch_shapes=[
            pltpu.VMEM((rows, depth), bf16),
            pltpu.VMEM((slots, depth, tile), bf16),
            pltpu.SemaphoreType.DMA((slots + 1,)),
        ],
        compiler_params=pltpu.CompilerParams(vmem_limit_bytes=50 * MIB),
        cost_estimate=pl.CostEstimate(
            flops=4 * rows * depth * width, bytes_accessed=4 * depth * width, transcendentals=0
        ),
        name="stream",
    )(x, gate, up)


def join_kernel(own_ref, got_ref, sum_ref, *send_refs):
    block = sum_ref.shape[1]
    total = own_ref[...] + got_ref[...].astype(f32)
    sum_ref[...] = total[:, :block]
    for step, send_ref in enumerate(send_refs, 1):
        send_ref[...] = total[:, step * block : (step + 1) * block].astype(bf16)


def join(block, own, got):
    vmem = pl.BlockSpec(memory_space=pltpu.VMEM)
    _, half, width = own.shape
    away = half // block - 1
    return pl.pallas_call(
        join_kernel,
        out_shape=[jax.ShapeDtypeStruct((2, block, width), f32)]
        + [jax.ShapeDtypeStruct((2, block, width), bf16)] * away,
        in_specs=[vmem] * 2,
        out_specs=[vmem] * (1 + away),
        compiler_params=pltpu.CompilerParams(vmem_limit_bytes=8 * MIB),
        cost_estimate=pl.CostEstimate(flops=1, bytes_accessed=1, transcendentals=0),
        name="join",
    )(own, got)


def activate_kernel(own_ref, *refs):
    def total(p):
        sums = own_ref[p]
        for got_ref in refs[:-1]:
            sums += got_ref[p].astype(f32)
        return sums

    gate, up = total(0), total(1)
    refs[-1][...] = (gate / (1.0 + jnp.exp(-gate)) * up).astype(bf16)


def activate(own, gots):
    vmem = pl.BlockSpec(memory_space=pltpu.VMEM)
    return pl.pallas_call(
        activate_kernel,
        out_shape=jax.ShapeDtypeStruct(own.shape[1:], bf16),
        in_specs=[vmem] * (1 + len(gots)),
        out_specs=vmem,
        compiler_params=pltpu.CompilerParams(vmem_limit_bytes=8 * MIB),
        cost_estimate=pl.CostEstimate(flops=1, bytes_accessed=1, transcendentals=0),
        name="activate",
    )(own, *gots)


def fetch_kernel(down_ref, after_ref, out_ref, arrived):
    copy = pltpu.make_async_copy(down_ref.at[pl.ds(0, out_ref.shape[0])], out_ref, arrived)
    copy.start()
    copy.wait()


def fetch(down, after, rows):
    far = pl.BlockSpec(memory_space=pltpu.HBM)
    return pl.pallas_call(
        fetch_kernel,
        out_shape=jax.ShapeDtypeStruct((rows, down.shape[1]), bf16),
        in_specs=[far, pl.BlockSpec(memory_space=pl.ANY)],
        out_specs=pl.BlockSpec(memory_space=pltpu.VMEM),
        scratch_shapes=[pltpu.SemaphoreType.DMA(())],
        compiler_params=pltpu.CompilerParams(vmem_limit_bytes=40 * MIB),
        cost_estimate=pl.CostEstimate(flops=1, bytes_accessed=1, transcendentals=0),
        name="fetch",
    )(down, after)


def project_kernel(count, near_ref, down_ref, *refs):
    blocks, (total_ref, hidden, early, held, arrived) = refs[:-5], refs[-5:]
    pieces, depth, columns = held.shape
    near = near_ref.shape[0]

    def bring(i):
        source = down_ref.at[pl.ds(near + i * depth, depth)]
        return pltpu.make_async_copy(source, held.at[i], arrived.at[i])

    for i in range(pieces):
        bring(i).start()
    me = lax.axis_index("replica")
    chips = count // 2
    start = 0
    for c in range(len(blocks) // count):
        parts = blocks[c * count : (c + 1) * count]
        block, width = parts[0].shape
        for nth, ref in enumerate(parts):
            chip = (me // 2 + nth % chips) % chips
            at = (chip * 2 + (me + nth // chips) % 2) * block
            hidden[pl.ds(pl.multiple_of(at, 16), block), start : start + width] = ref[...]
        start += width
    cuts = [slice(at, min(at + TILE, columns)) for at in range(0, columns, TILE)]
    for cut in cuts:
        early[:, cut] = dot(hidden[:, :near], near_ref[:, cut])
    for i in range(pieces):
        bring(i).wait()
    for cut in cuts:
        late = dot(hidden[:, near:], held[:, :, cut].reshape(pieces * depth, -1))
        total_ref[:, cut] = (early[:, cut] + late).astype(bf16)


def project(chunks, near, down):
    count = len(chunks[0])
    rows = count * chunks[0][0].shape[0]
    vmem = pl.BlockSpec(memory_space=pltpu.VMEM)
    far = pl.BlockSpec(memory_space=pltpu.HBM)
    blocks = [value for chunk in chunks for value in chunk]
    piece = PIECE if (down.shape[0] - near.shape[0]) % PIECE == 0 else PIECE // 2
    pieces = (down.shape[0] - near.shape[0]) // piece
    return pl.pallas_call(
        functools.partial(project_kernel, count),
        out_shape=jax.ShapeDtypeStruct((rows, down.shape[1]), bf16),
        in_specs=[vmem, far] + [vmem] * len(blocks),
        out_specs=vmem,
        scratch_shapes=[
            pltpu.VMEM((rows, down.shape[0]), bf16),
            pltpu.VMEM((rows, down.shape[1]), f32),
            pltpu.VMEM((pieces, piece, down.shape[1]), bf16),
            pltpu.SemaphoreType.DMA((pieces,)),
        ],
        compiler_params=pltpu.CompilerParams(vmem_limit_bytes=40 * MIB),
        cost_estimate=pl.CostEstimate(
            flops=2 * rows * down.size, bytes_accessed=2 * down.size, transcendentals=0
        ),
        name="project",
    )(near, down, *blocks)


def shards(
    tokens, gate_matrix, up_matrix, down_weight, adapter_down, adapter_up, adapter_ids, adapter_slot
):
    replicas, depth = lax.axis_size("replica"), lax.axis_size("tensor")
    chips = replicas // 2
    rows = tokens.shape[0]
    block = rows // replicas
    half = rows // 2
    units = gate_matrix.shape[1]

    pieces = [tokens, core_swap(tokens, replicas)]
    for step in range(1, chips):
        for flip in range(2):
            pieces.append(from_chip(tokens, replicas, step, flip))

    def sources(me):
        far = [((me + 2 * step) % replicas, flip) for step in range(1, chips) for flip in range(2)]
        near = [(me, 0), (me, 1)]
        return [at + flip * (1 - 2 * (at % 2)) for at, flip in near + far]

    widths = CHUNKS if sum(CHUNKS) == units else (units,)
    base, pieces[0] = stream(tokens, gate_matrix, up_matrix, block, chips, 0, units)
    expand = adapter_up.reshape(-1, units)
    spread, *parts = shrink_rows(
        pieces, sources, block, adapter_ids, adapter_slot, adapter_down, expand, base, widths[0]
    )
    if len(widths) > 1:
        parts += widen(spread, expand, base, widths[0], widths[0], widths[1:])
    sums = []
    for own, away in zip(parts[::2], parts[1::2]):
        own, *sends = join(block, own, core_swap(away, replicas))
        gots = [from_chip(send, replicas, chips - step) for step, send in enumerate(sends, 1)]
        sums.append((own, gots))
    chunks = []
    near = fetch(down_weight, sums[-1][0], units * 3 // 5)
    own, gots = sums[0]
    near, *gots = lax.optimization_barrier((near, *gots))
    sums[0] = own, gots
    for own, gots in sums:
        hidden = activate(own, gots)
        blocks = [hidden] + [from_chip(hidden, replicas, step) for step in range(1, chips)]
        chunks.append(blocks + [core_swap(value, replicas) for value in blocks])
    total = project(chunks, near, down_weight)
    reach = 1
    while reach < depth:
        pairs = [(i, i ^ (2 * reach - 1)) for i in range(depth)]
        total = (total.astype(f32) + lax.ppermute(total, "tensor", pairs).astype(f32)).astype(bf16)
        reach *= 2
    return total


def solution(mesh):
    placed = (
        P("groups", "replica"),
        P("replica", "tensor"),
        P("replica", "tensor"),
        P("tensor", "replica"),
        P("replica", None, None, None),
        P("replica", None, None, "tensor"),
        P("groups"),
        P("groups"),
    )
    return jax.shard_map(
        shards, mesh=mesh, in_specs=placed, out_specs=P("groups", "replica"), check_vma=False
    )
```
